32 devices in a mesh: ia: 2 (over x), ja: 4 (over y, core), ka: 4 (over z).
Axes of the slice: x: 2, y: 2, z: 4, core: 2. Of those that a mesh axis runs over, the one named last changes fastest.
Arguments:
- pre_act: bfloat16 [1024, 24576], P('ia', ('ja', 'ka')), may hold values from -6 to 6
- down_weight: bfloat16 [6144, 24576], P(('ka', 'ia'), 'ja'), may hold values from -0.0546875 to 0.0546875
- grad_out: bfloat16 [1024, 6144], P('ia', ('ka', 'ja')), may hold values from -6 to 6
Outputs:
- output: bfloat16 [1024, 6144], P('ia', ('ka', 'ja'))
- grad_pre: bfloat16 [1024, 24576], P('ia', ('ja', 'ka'))
- grad_weight: bfloat16 [6144, 24576], P(('ka', 'ia'), 'ja')
The draws below stay inside these ranges and needn't reach their ends.
All inputs are finite; a program needn't handle non-finite values.
Results may differ from the reference program's by a relative error of at most 0.02.
Values may be sent and summed in bfloat16 or wider, within the bound.
A program may use at most 128 MiB of HBM per device.

```python
import jax
import jax.numpy as jnp
from jax import lax

D = 6144
FF = 24576
TOK_DEV = 512
TOKENS = 1024
N_IA = 2
N_KA = 4


def strengthened(result, stream_key, source, target, parts, factor):
    def block_of(dim):
        return (jnp.arange(result.shape[dim]) // (result.shape[dim] // parts)).reshape((-1,) + (1,) * (result.ndim - 1 - dim))

    one_side = jax.random.permutation(stream_key, parts)[block_of(target)]
    far = (block_of(target) + parts // 2) % parts
    return jnp.where((block_of(source) == one_side) | (block_of(source) == far), factor * result, result)


def levels(key, extent, split, least, high):
    def one(dim, parts):
        steps = jax.random.uniform(jax.random.fold_in(jax.random.fold_in(key, 6), dim), (parts,), jnp.float32, least / len(split), high / len(split))
        return jnp.repeat(jnp.exp(steps), extent[dim] // parts).reshape((-1,) + (1,) * (len(extent) - dim - 1))

    gain = one(*split[0])
    for cut in split[1:]:
        gain = gain * one(*cut)
    return gain


def bell_draw(stream_key, shape, scale, bound, split=(), held_as=jnp.bfloat16):
    result = scale * jax.random.normal(stream_key, shape, jnp.float32)
    if split:
        result = result * levels(stream_key, shape, split, -0.22, 0.18)
    return jnp.clip(result, -bound, bound).astype(held_as)


def noise_with(stream_key, shape, deviation, bound, cuts, heavy, dtype=jnp.bfloat16):
    result = deviation * jax.random.normal(stream_key, shape, jnp.float32)
    if cuts:
        result = result * levels(stream_key, shape, cuts, -0.22, 0.18)
    return jnp.clip(strengthened(result, jax.random.fold_in(stream_key, 3), *heavy), -bound, bound).astype(dtype)


def setup_inputs(seed: int = 0) -> dict:
    streams_of = jax.random.split(jax.random.key(seed), 4)
    return {
        "pre_act": bell_draw(streams_of[0], (TOKENS, FF), 1.0, 6.0, ((0, 2), (1, 16))),
        "down_weight": noise_with(streams_of[1], (D, FF), FF ** -0.5, 0.0546875, ((0, 8), (1, 4)), (0, 1, 8, 2.0)),
        "grad_out": noise_with(streams_of[2], (TOKENS, D), 1.0, 6.0, ((0, 2), (1, 16)), (0, 1, 16, 2.0)),
    }


coeff = 0.7978845608028654


def gelu_value(v):
    return 0.5 * v * (1.0 + jnp.tanh(coeff * (v + 0.044715 * v * v * v)))


def gelu_slope(v):
    tval = jnp.tanh(coeff * (v + 0.044715 * v * v * v))
    return 0.5 * (1.0 + tval) + 0.5 * v * (1.0 - tval * tval) * coeff * (1.0 + 3.0 * 0.044715 * v * v)


def reference(pre_act, down_weight, grad_out):
    pre32 = pre_act.astype(jnp.float32)
    hidden = gelu_value(pre32).astype(jnp.bfloat16)
    output = lax.dot_general(hidden, down_weight, (((1,), (1,)), ((), ())), preferred_element_type=jnp.float32).astype(jnp.bfloat16)
    width = D // N_KA
    grad_hidden = jnp.zeros((TOKENS, FF), jnp.float32)
    for block in range(N_KA):
        cols = grad_out[:, block * width:(block + 1) * width]
        wrows = down_weight[block * width:(block + 1) * width]
        part = jnp.dot(cols, wrows, preferred_element_type=jnp.float32)
        grad_hidden = grad_hidden + part.astype(jnp.bfloat16).astype(jnp.float32)
    grad_pre = (grad_hidden * gelu_slope(pre32)).astype(jnp.bfloat16)
    grad_weight = jnp.zeros((D, FF), jnp.float32)
    for block in range(N_IA):
        rows = hidden[block * TOK_DEV:(block + 1) * TOK_DEV]
        grows = grad_out[block * TOK_DEV:(block + 1) * TOK_DEV]
        part = lax.dot_general(grows, rows, (((0,), (0,)), ((), ())), preferred_element_type=jnp.float32)
        grad_weight = grad_weight + part.astype(jnp.bfloat16).astype(jnp.float32)
    return output, grad_pre, grad_weight.astype(jnp.bfloat16)
```

```python
import jax
import jax.numpy as jnp
from jax import lax
from jax.sharding import PartitionSpec as P

coeff = 0.7978845608028654


def gelu_value(v):
    return 0.5 * v * (1.0 + jnp.tanh(coeff * (v + 0.044715 * v * v * v)))


def gelu_slope(v):
    tval = jnp.tanh(coeff * (v + 0.044715 * v * v * v))
    return 0.5 * (1.0 + tval) + 0.5 * v * (1.0 - tval * tval) * coeff * (
        1.0 + 3.0 * 0.044715 * v * v
    )


def shards(pre_act, down_weight, grad_out):
    pre32 = pre_act.astype(jnp.float32)
    pre_block = lax.all_gather(pre_act, "ka", axis=1, tiled=True)
    hidden = gelu_value(pre_block.astype(jnp.float32)).astype(jnp.bfloat16)
    grad_block = lax.all_gather(grad_out, "ja", axis=1, tiled=True)
    weight_block = lax.all_gather(down_weight, "ia", axis=0, tiled=True)
    out_terms = lax.dot_general(
        hidden, weight_block, (((1,), (1,)), ((), ())), preferred_element_type=jnp.float32
    )
    hidden_terms = jnp.dot(grad_block, weight_block, preferred_element_type=jnp.float32)
    output = lax.psum_scatter(out_terms.astype(jnp.bfloat16), "ja", scatter_dimension=1, tiled=True)
    grad_hidden = lax.psum_scatter(
        hidden_terms.astype(jnp.bfloat16), "ka", scatter_dimension=1, tiled=True
    ).astype(jnp.float32)
    grad_pre = (grad_hidden * gelu_slope(pre32)).astype(jnp.bfloat16)
    weight_terms = lax.dot_general(
        grad_block, hidden, (((0,), (0,)), ((), ())), preferred_element_type=jnp.float32
    )
    grad_weight = lax.psum_scatter(
        weight_terms.astype(jnp.bfloat16), "ia", scatter_dimension=0, tiled=True
    )
    return (output, grad_pre, grad_weight)


def stationary(pre_act, down_weight, grad_out):
    pre32 = pre_act.astype(jnp.float32)
    grad_block = lax.all_gather(grad_out, "ja", axis=1, tiled=True)
    grad_block = lax.all_to_all(grad_block, "ia", split_axis=1, concat_axis=0, tiled=True)
    pre_block = lax.all_gather(pre_act, "ka", axis=1, tiled=True)
    pre_block = lax.all_gather(pre_block, "ia", axis=0, tiled=True)
    hidden_terms = jnp.dot(grad_block, down_weight, preferred_element_type=jnp.float32)
    grad_hidden = lax.psum_scatter(
        hidden_terms.astype(jnp.bfloat16), "ia", scatter_dimension=0, tiled=True
    )
    grad_hidden = lax.psum_scatter(grad_hidden, "ka", scatter_dimension=1, tiled=True)
    hidden = gelu_value(pre_block.astype(jnp.float32)).astype(jnp.bfloat16)
    out_terms = lax.dot_general(
        hidden, down_weight, (((1,), (1,)), ((), ())), preferred_element_type=jnp.float32
    )
    out_terms = lax.all_to_all(
        out_terms.astype(jnp.bfloat16), "ia", split_axis=0, concat_axis=1, tiled=True
    )
    output = lax.psum_scatter(out_terms, "ja", scatter_dimension=1, tiled=True)
    grad_weight = lax.dot_general(
        grad_block, hidden, (((0,), (0,)), ((), ())), preferred_element_type=jnp.float32
    ).astype(jnp.bfloat16)
    grad_pre = (grad_hidden.astype(jnp.float32) * gelu_slope(pre32)).astype(jnp.bfloat16)
    return (output, grad_pre, grad_weight)


def pick(n_ia):
    def chosen(pre_act, down_weight, grad_out):
        if n_ia * down_weight.shape[0] > n_ia * pre_act.shape[0]:
            return stationary(pre_act, down_weight, grad_out)
        return shards(pre_act, down_weight, grad_out)

    return chosen


def solution(mesh):
    placed = (P("ia", ("ja", "ka")), P(("ka", "ia"), "ja"), P("ia", ("ka", "ja")))
    return jax.shard_map(
        pick(mesh.shape["ia"]),
        mesh=mesh,
        in_specs=placed,
        out_specs=(P("ia", ("ka", "ja")), P("ia", ("ja", "ka")), P(("ka", "ia"), "ja")),
        check_vma=False,
    )
```

```python
import functools

import jax
import jax.numpy as jnp
from jax import lax
from jax.experimental import pallas as pl
from jax.experimental.pallas import tpu as pltpu
from jax.sharding import PartitionSpec as P

MESH = pl.DeviceIdType.MESH
coeff = 0.7978845608028654


def gelu_value(v):
    return 0.5 * v * (1.0 + jnp.tanh(coeff * (v + 0.044715 * v * v * v)))


def gelu_slope(v):
    tval = jnp.tanh(coeff * (v + 0.044715 * v * v * v))
    return 0.5 * (1.0 + tval) + 0.5 * v * (1.0 - tval * tval) * coeff * (
        1.0 + 3.0 * 0.044715 * v * v
    )


def shards(pre_act, down_weight, grad_out):
    pre32 = pre_act.astype(jnp.float32)
    pre_block = lax.all_gather(pre_act, "ka", axis=1, tiled=True)
    hidden = gelu_value(pre_block.astype(jnp.float32)).astype(jnp.bfloat16)
    grad_block = lax.all_gather(grad_out, "ja", axis=1, tiled=True)
    weight_block = lax.all_gather(down_weight, "ia", axis=0, tiled=True)
    out_terms = lax.dot_general(
        hidden, weight_block, (((1,), (1,)), ((), ())), preferred_element_type=jnp.float32
    )
    hidden_terms = jnp.dot(grad_block, weight_block, preferred_element_type=jnp.float32)
    output = lax.psum_scatter(out_terms.astype(jnp.bfloat16), "ja", scatter_dimension=1, tiled=True)
    grad_hidden = lax.psum_scatter(
        hidden_terms.astype(jnp.bfloat16), "ka", scatter_dimension=1, tiled=True
    ).astype(jnp.float32)
    grad_pre = (grad_hidden * gelu_slope(pre32)).astype(jnp.bfloat16)
    weight_terms = lax.dot_general(
        grad_block, hidden, (((0,), (0,)), ((), ())), preferred_element_type=jnp.float32
    )
    grad_weight = lax.psum_scatter(
        weight_terms.astype(jnp.bfloat16), "ia", scatter_dimension=0, tiled=True
    )
    return (output, grad_pre, grad_weight)


def kernel(
    X, J, Z, ra, ct, rt,
    pre, w_hbm, go, out, gp, gw,
    w, pre_all, g, gt, part, r1, rza, rzb, rf, outp, outr, outx, gwt,
    loc, gws, go_s, go_r, gb_s, gb_r, ag_s, ag_r, r1_s, r1_r, ra_s, ra_r, rb_s, rb_r,
    rf_s, rf_r, op_s, op_r, ox_s, ox_r,
):
    x, j, z = lax.axis_index("ia"), lax.axis_index("ja"), lax.axis_index("ka")
    px = 1 - x
    _, _, tok, cols = pre_all.shape
    fc = go.shape[1]
    nb = J // X
    home, b = lax.div(j, nb) == x, lax.rem(j, nb)
    bcols = pl.ds(pl.multiple_of(b * fc, fc), fc)
    to_px, to_right, to_left = {"ia": px}, {"ka": z + 1}, {"ka": z - 1}
    has_left, has_right = z > 0, z < Z - 1
    rows = (pl.ds(0, ra), pl.ds(ra, tok - ra))

    def remote(src, dst, ss, rs, dev):
        return pltpu.make_async_remote_copy(
            src_ref=src, dst_ref=dst, send_sem=ss, recv_sem=rs, device_id=dev, device_id_type=MESH
        )

    def got(dst, rs):
        remote(dst, dst, rs, rs, to_px).wait_recv()

    barrier = pltpu.get_barrier_semaphore()

    def greet(dev):
        pl.semaphore_signal(barrier, inc=1, device_id=dev, device_id_type=MESH)

    greet(to_px)
    for q in range(1, J):
        greet({"ja": lax.rem(j + q, J)})
    pl.when(has_right)(lambda: greet(to_right))
    pl.when(has_left)(lambda: greet(to_left))
    w_in = pltpu.make_async_copy(w_hbm, w, loc.at[0])
    w_in.start()
    own_in = pltpu.make_async_copy(pre, pre_all.at[x, z], loc.at[1])
    own_in.start()
    pre_in = pltpu.make_async_copy(pre, gp, loc.at[2])
    pre_in.start()
    pl.semaphore_wait(barrier, J + has_right.astype(jnp.int32) + has_left.astype(jnp.int32))

    ag_sent = []
    devs = (to_right, to_left, to_px)

    def ag_send(p, xs, s, t, cond, own=False):
        def copy():
            src = pre.at[rows[p]] if own else pre_all.at[xs, s, rows[p]]
            return remote(
                src, pre_all.at[xs, s, rows[p]], ag_s.at[p, xs, s, t], ag_r.at[p, xs, s], devs[t]
            )

        pl.when(cond)(lambda: copy().start())
        ag_sent.append((cond, copy))

    def ag_got(p, xs, s):
        got(pre_all.at[xs, s, rows[p]], ag_r.at[p, xs, s])

    always = z >= 0

    def go_copy():
        return remote(go, g.at[x, :, bcols], go_s.at[0], go_r.at[0], to_px)

    go_in = pltpu.make_async_copy(go, g.at[x, :, bcols], loc.at[3])
    pl.when(jnp.logical_not(home))(lambda: go_copy().start())
    pl.when(home)(lambda: go_in.start())
    ag_send(1, x, z, 2, always, True)
    ag_send(0, x, z, 0, has_right, True)
    ag_send(0, x, z, 1, has_left, True)
    ag_send(0, x, z, 2, always, True)
    ag_send(1, x, z, 0, has_right, True)
    ag_send(1, x, z, 1, has_left, True)

    def gb_copy(q):
        return remote(
            g.at[:, :, bcols], g.at[:, :, bcols], gb_s.at[q], gb_r.at[b], {"ja": lax.rem(j + q, J)}
        )

    @pl.when(home)
    def _():
        go_in.wait()
        got(g.at[px, :, bcols], go_r.at[0])
        for q in range(1, J):
            gb_copy(q).start()

    ag_got(1, px, z)
    ag_send(1, px, z, 0, has_right)
    ag_send(1, px, z, 1, has_left)

    def ag_step(k):
        for s, came, t, more in ((z - k, z >= k, 0, has_right), (z + k, z + k < Z, 1, has_left)):
            pl.when(came)(lambda s=s: ag_got(0, x, s))
            ag_send(0, x, s, 2, came)
            ag_send(0, x, s, t, jnp.logical_and(came, more))
            for xs in (x, px):
                pl.when(came)(lambda s=s, xs=xs: ag_got(1, xs, s))
                ag_send(1, xs, s, t, jnp.logical_and(came, more))

    ag_step(1)

    for bb in range(nb):
        view = g.at[:, :, pl.ds(bb * fc, fc)]
        pl.when(j != nb * x + bb)(lambda view=view, bb=bb: got(view, gb_r.at[bb]))
    w_in.wait()

    def r1_copy(d):
        return remote(part.at[px, d, rows[0]], r1.at[d], r1_s.at[d], r1_r.at[d], to_px)

    def terms(xs, i):
        d = jnp.where(z >= Z // 2, i, Z - 1 - i)

        def tile(c, carry):
            wide = pl.ds(pl.multiple_of(d * cols + c * ct, ct), ct)
            at = pl.ds(pl.multiple_of(c * ct, ct), ct)
            value = jnp.dot(g[xs], w[:, wide], preferred_element_type=jnp.float32)
            part[xs, d, :, at] = value.astype(jnp.bfloat16)
            return carry

        lax.fori_loop(0, cols // ct, tile, 0)
        return d

    def terms_px(i, carry):
        r1_copy(terms(px, i)).start()
        return carry

    def terms_x(i, carry):
        terms(x, i)
        return carry

    lax.fori_loop(0, Z, terms_px, 0)
    lax.fori_loop(0, Z, terms_x, 0)

    def add(dst, src, count):
        def tile(r, carry):
            at = pl.ds(pl.multiple_of(r * 16, 16), 16)
            value = dst[at].astype(jnp.float32) + src[at].astype(jnp.float32)
            dst[at] = value.astype(jnp.bfloat16)
            return carry

        lax.fori_loop(0, count // 16, tile, 0)

    rs_sent = []

    def take_a(d, slot):
        got(rza.at[slot], ra_r.at[slot])
        add(part.at[x, d, rows[0]], rza.at[slot], ra)

    def take_b(xs, d, slot):
        got(rzb.at[xs, slot], rb_r.at[xs, slot])
        add(part.at[xs, d, rows[1]], rzb.at[xs, slot], tok - ra)

    def take_1(d):
        got(r1.at[d], r1_r.at[d])
        add(part.at[x, d, rows[0]], r1.at[d], ra)

    def rs_step(i):
        for d, cond, more, slot, dev in (
            (Z - 1 - i, Z - 1 - i > z, has_left, Z - 1 - i, to_right),
            (i, i < z, has_right, jnp.where(z == i + 1, Z, i), to_left),
        ):
            for xs in (px, x):

                def copy_b(xs=xs, d=d, slot=slot, dev=dev):
                    return remote(
                        part.at[xs, d, rows[1]], rzb.at[xs, slot],
                        rb_s.at[xs, d], rb_r.at[xs, slot], dev,
                    )

                pl.when(jnp.logical_and(cond, more))(lambda xs=xs, d=d: take_b(xs, d, d))
                pl.when(cond)(lambda copy_b=copy_b: copy_b().start())
                rs_sent.append((cond, copy_b))

            def copy_a(d=d, slot=slot, dev=dev):
                return remote(
                    part.at[x, d, rows[0]], rza.at[slot], ra_s.at[d], ra_r.at[slot], dev
                )

            pl.when(cond)(lambda d=d: take_1(d))
            pl.when(jnp.logical_and(cond, more))(lambda d=d: take_a(d, d))
            pl.when(cond)(lambda copy_a=copy_a: copy_a().start())
            rs_sent.append((cond, copy_a))

    mid = Z - 2
    for k in range(2, Z):
        ag_step(k)
        if k - 2 < mid:
            rs_step(k - 2)

    for s in range(Z):
        pl.when(z != s)(lambda s=s: ag_got(0, px, s))
    ag_got(0, px, z)
    own_in.wait()
    for cond, copy in ag_sent:
        pl.when(cond)(lambda copy=copy: copy().wait_send())

    def act(n, carry):
        xs, rest = lax.div(n, Z * (tok // 16)), lax.rem(n, Z * (tok // 16))
        s, r = lax.div(rest, tok // 16), lax.rem(rest, tok // 16)
        at = pl.ds(pl.multiple_of(r * 16, 16), 16)
        pre_all[xs, s, at] = gelu_value(pre_all[xs, s, at].astype(jnp.float32)).astype(jnp.bfloat16)
        return carry

    lax.fori_loop(0, X * Z * (tok // 16), act, 0)

    def out_tile(n, carry):
        xs, r = lax.div(n, tok // rt), lax.rem(n, tok // rt)
        at = pl.ds(pl.multiple_of(r * rt, rt), rt)
        acc = None
        for s in range(Z):
            term = lax.dot_general(
                pre_all[xs, s, at], w[:, s * cols : (s + 1) * cols], (((1,), (1,)), ((), ())),
                preferred_element_type=jnp.float32,
            )
            acc = term if acc is None else acc + term
        for bb in range(nb):
            outp[bb, xs, at] = acc[:, bb * fc : (bb + 1) * fc].astype(jnp.bfloat16)
        return carry

    lax.fori_loop(0, X * (tok // rt), out_tile, 0)

    def op_copy(bb):
        jd = nb * x + bb
        q = lax.rem(j - jd - 1 + J, J)
        return remote(outp.at[bb], outr.at[q], op_s.at[bb], op_r.at[q], {"ja": jd})

    for bb in range(nb):
        pl.when(j != nb * x + bb)(lambda bb=bb: op_copy(bb).start())

    for i in range(mid, Z - 1):
        rs_step(i)

    for xs in range(X):
        gt[:, xs * tok : (xs + 1) * tok] = g[xs].T

    n_tiles = Z * (cols // ct)

    def gw_copy(n, slot):
        wide = pl.ds(pl.multiple_of(n * ct, ct), ct)
        return pltpu.make_async_copy(gwt.at[slot], gw.at[:, wide], gws.at[slot])

    def gw_tile(n, carry):
        slot = lax.rem(n, 2)
        s, c = lax.div(n, cols // ct), lax.rem(n, cols // ct)
        at = pl.ds(pl.multiple_of(c * ct, ct), ct)
        pl.when(n >= 2)(lambda: gw_copy(n - 2, slot).wait())
        acc = None
        for xs in range(X):
            term = jnp.dot(
                gt[:, xs * tok : (xs + 1) * tok], pre_all[xs, s, :, at],
                preferred_element_type=jnp.float32,
            )
            acc = term if acc is None else acc + term
        gwt[slot] = acc.astype(jnp.bfloat16)
        gw_copy(n, slot).start()
        return carry

    lax.fori_loop(0, n_tiles, gw_tile, 0)

    def rf_copy():
        return remote(part.at[px, z, rows[1]], rf, rf_s.at[0], rf_r.at[0], to_px)

    for xs in (px, x):
        pl.when(has_left)(lambda xs=xs: take_b(xs, z, z))
        pl.when(has_right)(lambda xs=xs: take_b(xs, z, Z))
        if xs is px:
            rf_copy().start()
    take_1(z)
    pl.when(has_left)(lambda: take_a(z, z))
    pl.when(has_right)(lambda: take_a(z, Z))

    def ox_copy():
        return remote(outp.at[b, px], outx, ox_s.at[0], ox_r.at[0], to_px)

    @pl.when(home)
    def _():
        for q in range(J - 1):
            got(outr.at[q], op_r.at[q])

        def total(xs, r):
            at = pl.ds(pl.multiple_of(r * 16, 16), 16)
            value = outp[b, xs, at].astype(jnp.float32)
            for q in range(J - 1):
                value = value + outr[q, xs, at].astype(jnp.float32)
            return at, value.astype(jnp.bfloat16)

        def far(r, carry):
            at, value = total(px, r)
            outp[b, px, at] = value
            return carry

        def near(r, carry):
            at, value = total(x, r)
            out[at] = value
            return carry

        lax.fori_loop(0, tok // 16, far, 0)
        ox_copy().start()
        lax.fori_loop(0, tok // 16, near, 0)

    pre_in.wait()

    def slope(r, carry):
        at = pl.ds(pl.multiple_of(r * 16, 16), 16)
        value = part[x, z, at].astype(jnp.float32) * gelu_slope(gp[at].astype(jnp.float32))
        gp[at] = value.astype(jnp.bfloat16)
        return carry

    lax.fori_loop(0, ra // 16, slope, 0)
    got(rf, rf_r.at[0])
    add(part.at[x, z, rows[1]], rf, tok - ra)
    lax.fori_loop(ra // 16, tok // 16, slope, 0)

    @pl.when(jnp.logical_not(home))
    def _():
        got(outx, ox_r.at[0])
        out[...] = outx[...]
        go_copy().wait_send()

    @pl.when(home)
    def _():
        ox_copy().wait_send()
        for q in range(1, J):
            gb_copy(q).wait_send()

    for bb in range(nb):
        pl.when(j != nb * x + bb)(lambda bb=bb: op_copy(bb).wait_send())
    rf_copy().wait_send()
    for d in range(Z):
        r1_copy(d).wait_send()
    for cond, copy in rs_sent:
        pl.when(cond)(lambda copy=copy: copy().wait_send())
    for n in range(max(n_tiles - 2, 0), n_tiles):
        gw_copy(n, n % 2).wait()


def stationary(X, J, Z, pre_act, down_weight, grad_out):
    tok, cols = pre_act.shape
    feats, hid = down_weight.shape
    fc = grad_out.shape[1]
    ra = tok * 9 // 16 // 16 * 16
    rb = tok - ra
    ct = 512 if cols % 512 == 0 else 128
    rt = 256 if tok % 256 == 0 else tok
    nb = J // X
    half = jnp.bfloat16
    dma = pltpu.SemaphoreType.DMA
    anywhere = pl.BlockSpec(memory_space=pl.ANY)
    vmem = pl.BlockSpec(memory_space=pltpu.VMEM)
    return pl.pallas_call(
        functools.partial(kernel, X, J, Z, ra, ct, rt),
        out_shape=(
            jax.ShapeDtypeStruct((tok, fc), half),
            jax.ShapeDtypeStruct((tok, cols), half),
            jax.ShapeDtypeStruct((feats, hid), half),
        ),
        in_specs=[anywhere] * 3,
        out_specs=(vmem, vmem, anywhere),
        scratch_shapes=[
            pltpu.VMEM((feats, hid), half),
            pltpu.VMEM((X, Z, tok, cols), half),
            pltpu.VMEM((X, tok, nb * fc), half),
            pltpu.VMEM((nb * fc, X * tok), half),
            pltpu.VMEM((X, Z, tok, cols), half),
            pltpu.VMEM((Z, ra, cols), half),
            pltpu.VMEM((Z + 1, ra, cols), half),
            pltpu.VMEM((X, Z + 1, rb, cols), half),
            pltpu.VMEM((rb, cols), half),
            pltpu.VMEM((nb, X, tok, fc), half),
            pltpu.VMEM((J - 1, X, tok, fc), half),
            pltpu.VMEM((tok, fc), half),
            pltpu.VMEM((2, feats, ct), half),
            dma((4,)), dma((2,)), dma((1,)), dma((1,)), dma((J,)), dma((nb,)),
            dma((2, X, Z, 3)), dma((2, X, Z)), dma((Z,)), dma((Z,)), dma((Z,)), dma((Z + 1,)),
            dma((X, Z)), dma((X, Z + 1)), dma((1,)), dma((1,)), dma((nb,)), dma((J,)),
            dma((1,)), dma((1,)),
        ],
        compiler_params=pltpu.CompilerParams(
            collective_id=0, has_side_effects=True, vmem_limit_bytes=63 * 2**20
        ),
    )(pre_act, down_weight, grad_out)


def pick(n_ia, n_ja, n_ka):
    def chosen(pre_act, down_weight, grad_out):
        if n_ia == 2 and down_weight.shape[0] > pre_act.shape[0]:
            return stationary(n_ia, n_ja, n_ka, pre_act, down_weight, grad_out)
        return shards(pre_act, down_weight, grad_out)

    return chosen


def solution(mesh):
    placed = (P("ia", ("ja", "ka")), P(("ka", "ia"), "ja"), P("ia", ("ka", "ja")))
    return jax.shard_map(
        pick(mesh.shape["ia"], mesh.shape["ja"], mesh.shape["ka"]),
        mesh=mesh,
        in_specs=placed,
        out_specs=(P("ia", ("ka", "ja")), P("ia", ("ja", "ka")), P(("ka", "ia"), "ja")),
        check_vma=False,
    )
```

```python
import functools

import jax
import jax.numpy as jnp
from jax import lax
from jax.experimental import pallas as pl
from jax.experimental.pallas import tpu as pltpu
from jax.sharding import PartitionSpec as P

MESH = pl.DeviceIdType.MESH
coeff = 0.7978845608028654


def gelu_value(v):
    return 0.5 * v * (1.0 + jnp.tanh(coeff * (v + 0.044715 * v * v * v)))


def gelu_slope(v):
    tval = jnp.tanh(coeff * (v + 0.044715 * v * v * v))
    return 0.5 * (1.0 + tval) + 0.5 * v * (1.0 - tval * tval) * coeff * (
        1.0 + 3.0 * 0.044715 * v * v
    )


def shards(pre_act, down_weight, grad_out):
    pre32 = pre_act.astype(jnp.float32)
    pre_block = lax.all_gather(pre_act, "ka", axis=1, tiled=True)
    hidden = gelu_value(pre_block.astype(jnp.float32)).astype(jnp.bfloat16)
    grad_block = lax.all_gather(grad_out, "ja", axis=1, tiled=True)
    weight_block = lax.all_gather(down_weight, "ia", axis=0, tiled=True)
    out_terms = lax.dot_general(
        hidden, weight_block, (((1,), (1,)), ((), ())), preferred_element_type=jnp.float32
    )
    hidden_terms = jnp.dot(grad_block, weight_block, preferred_element_type=jnp.float32)
    output = lax.psum_scatter(out_terms.astype(jnp.bfloat16), "ja", scatter_dimension=1, tiled=True)
    grad_hidden = lax.psum_scatter(
        hidden_terms.astype(jnp.bfloat16), "ka", scatter_dimension=1, tiled=True
    ).astype(jnp.float32)
    grad_pre = (grad_hidden * gelu_slope(pre32)).astype(jnp.bfloat16)
    weight_terms = lax.dot_general(
        grad_block, hidden, (((0,), (0,)), ((), ())), preferred_element_type=jnp.float32
    )
    grad_weight = lax.psum_scatter(
        weight_terms.astype(jnp.bfloat16), "ia", scatter_dimension=0, tiled=True
    )
    return (output, grad_pre, grad_weight)


def kernel(
    X, J, Z, ra, ct, rt,
    pre, w_hbm, go, out, gp, gw,
    w, pre_all, g, gt, part, r1, rza, rzb, rf, outp, outr, outx, gwt,
    loc, gws, go_s, go_r, gb_s, gb_r, ag_s, ag_r, r1_s, r1_r, ra_s, ra_r, rb_s, rb_r,
    rf_s, rf_r, op_s, op_r, ox_s, ox_r,
):
    x, j, z = lax.axis_index("ia"), lax.axis_index("ja"), lax.axis_index("ka")
    px = 1 - x
    _, _, tok, cols = pre_all.shape
    fc = go.shape[1]
    nb = J // X
    home, b = lax.div(j, nb) == x, lax.rem(j, nb)
    bcols = pl.ds(pl.multiple_of(b * fc, fc), fc)
    to_px, to_right, to_left = {"ia": px}, {"ka": z + 1}, {"ka": z - 1}
    has_left, has_right = z > 0, z < Z - 1
    rows = (pl.ds(0, ra), pl.ds(ra, tok - ra))

    def remote(src, dst, ss, rs, dev):
        return pltpu.make_async_remote_copy(
            src_ref=src, dst_ref=dst, send_sem=ss, recv_sem=rs, device_id=dev, device_id_type=MESH
        )

    def got(dst, rs):
        remote(dst, dst, rs, rs, to_px).wait_recv()

    barrier = pltpu.get_barrier_semaphore()

    def greet(dev):
        pl.semaphore_signal(barrier, inc=1, device_id=dev, device_id_type=MESH)

    greet(to_px)
    for q in range(1, J):
        greet({"ja": lax.rem(j + q, J)})
    pl.when(has_right)(lambda: greet(to_right))
    pl.when(has_left)(lambda: greet(to_left))
    w_in = pltpu.make_async_copy(w_hbm, w, loc.at[0])
    w_in.start()
    own_in = pltpu.make_async_copy(pre, pre_all.at[x, z], loc.at[1])
    own_in.start()
    pre_in = pltpu.make_async_copy(pre, gp, loc.at[2])
    pre_in.start()
    pl.semaphore_wait(barrier, J + has_right.astype(jnp.int32) + has_left.astype(jnp.int32))

    ag_sent = {}
    devs = (to_right, to_left, to_px)

    def ag_send(p, xs, s, t, cond, own=False):
        def copy():
            src = pre.at[rows[p]] if own else pre_all.at[xs, s, rows[p]]
            return remote(
                src, pre_all.at[xs, s, rows[p]], ag_s.at[p, xs, s, t], ag_r.at[p, xs, s], devs[t]
            )

        pl.when(cond)(lambda: copy().start())
        ag_sent.setdefault((xs is x, id(s)), []).append((cond, copy))

    def ag_got(p, xs, s):
        got(pre_all.at[xs, s, rows[p]], ag_r.at[p, xs, s])

    always = z >= 0

    def go_copy():
        return remote(go, g.at[x, :, bcols], go_s.at[0], go_r.at[0], to_px)

    go_in = pltpu.make_async_copy(go, g.at[x, :, bcols], loc.at[3])
    pl.when(jnp.logical_not(home))(lambda: go_copy().start())
    pl.when(home)(lambda: go_in.start())
    ag_send(1, x, z, 2, always, True)
    ag_send(0, x, z, 0, has_right, True)
    ag_send(0, x, z, 1, has_left, True)
    ag_send(0, x, z, 2, always, True)
    ag_send(1, x, z, 0, has_right, True)
    ag_send(1, x, z, 1, has_left, True)

    mate = {"ja": j + 1 - 2 * lax.rem(j, 2)}
    across = {"ja": lax.rem(j + 2, J)}
    ocols = pl.ds(pl.multiple_of((nb - 1 - b) * fc, fc), fc)

    def gb_copy(h, n):
        view = g.at[h, :, bcols]
        return remote(view, view, gb_s.at[n, h], gb_r.at[n, h], (mate, across)[n])

    @pl.when(home)
    def _():
        go_in.wait()
        gb_copy(x, 1).start()
        gb_copy(x, 0).start()
        got(g.at[px, :, bcols], go_r.at[0])
        gb_copy(px, 1).start()
        gb_copy(px, 0).start()

    @pl.when(jnp.logical_not(home))
    def _():
        for h in (x, px):
            got(g.at[h, :, bcols], gb_r.at[1, h])
            gb_copy(h, 0).start()

    ag_got(1, px, z)
    ag_send(1, px, z, 0, has_right)
    ag_send(1, px, z, 1, has_left)

    def ag_step(k):
        sides = ((z - k, z >= k, 0, has_right), (z + k, z + k < Z, 1, has_left))
        for s, came, t, more in sides:
            pl.when(came)(lambda s=s: ag_got(0, x, s))
            ag_send(0, x, s, t, jnp.logical_and(came, more))
            ag_send(0, x, s, 2, came)
            for xs in (x, px):
                pl.when(came)(lambda s=s, xs=xs: ag_got(1, xs, s))
                ag_send(1, xs, s, t, jnp.logical_and(came, more))
        return [(s, came) for s, came, _, _ in sides]

    for h in (x, px):
        got(g.at[h, :, ocols], gb_r.at[0, h])
    w_in.wait()

    def r1_copy(d):
        return remote(part.at[px, d, rows[0]], r1.at[d], r1_s.at[d], r1_r.at[d], to_px)

    def far(i):
        d = 0
        for at in range(Z):
            d = d + jnp.where(z == at, sorted(range(Z), key=lambda o: -abs(o - at))[i], 0)
        return d

    def terms(xs, d):
        def tile(c, carry):
            wide = pl.ds(pl.multiple_of(d * cols + c * ct, ct), ct)
            at = pl.ds(pl.multiple_of(c * ct, ct), ct)
            value = jnp.dot(g[xs], w[:, wide], preferred_element_type=jnp.float32)
            part[xs, d, :, at] = value.astype(jnp.bfloat16)
            return carry

        lax.fori_loop(0, cols // ct, tile, 0)

    terms(px, far(0))
    r1_copy(far(0)).start()
    for i in range(1, Z):
        terms(px, far(i))
    for i in range(Z):
        terms(x, far(i))

    def add(dst, src, count):
        def tile(r, carry):
            at = pl.ds(pl.multiple_of(r * 16, 16), 16)
            value = dst[at].astype(jnp.float32) + src[at].astype(jnp.float32)
            dst[at] = value.astype(jnp.bfloat16)
            return carry

        lax.fori_loop(0, count // 16, tile, 0)

    rs_sent = []

    def take_a(d, slot):
        got(rza.at[slot], ra_r.at[slot])
        add(part.at[x, d, rows[0]], rza.at[slot], ra)

    def take_b(xs, d, slot):
        got(rzb.at[xs, slot], rb_r.at[xs, slot])
        add(part.at[xs, d, rows[1]], rzb.at[xs, slot], tok - ra)

    def take_1(d):
        got(r1.at[d], r1_r.at[d])
        add(part.at[x, d, rows[0]], r1.at[d], ra)

    def rs_way(right, i, cond):
        d = Z - 1 - i if right else i
        cond = jnp.logical_and(cond, d > z if right else d < z)
        more = has_left if right else has_right
        slot = d if right else jnp.where(z == i + 1, Z, i)
        dev = to_right if right else to_left

        def copy_b(xs):
            return remote(
                part.at[xs, d, rows[1]], rzb.at[xs, slot],
                rb_s.at[xs, d], rb_r.at[xs, slot], dev,
            )

        def copy_a():
            return remote(part.at[x, d, rows[0]], rza.at[slot], ra_s.at[d], ra_r.at[slot], dev)

        def part_b():
            for xs in (px, x):

                @pl.when(cond)
                def _():
                    pl.when(more)(lambda: take_b(xs, d, d))
                    copy_b(xs).start()

                rs_sent.append((cond, lambda xs=xs: copy_b(xs)))

        def part_a():
            @pl.when(cond)
            def _():
                take_1(d)
                pl.when(more)(lambda: take_a(d, d))
                copy_a().start()

            rs_sent.append((cond, copy_a))

        return part_b, part_a

    def both(way):
        way[0]()
        way[1]()

    def act(xs, s, cond):
        own = xs is x and s is z

        def tile(r, carry):
            at = pl.ds(pl.multiple_of(r * 16, 16), 16)
            value = gelu_value(pre_all[xs, s, at].astype(jnp.float32))
            pre_all[xs, s, at] = value.astype(jnp.bfloat16)
            return carry

        @pl.when(cond)
        def _():
            for to, copy in () if own else ag_sent[xs is x, id(s)]:
                pl.when(to)(lambda copy=copy: copy().wait_send())
            if xs is px:
                ag_got(0, px, s)
            elif own:
                own_in.wait()
            lax.fori_loop(0, tok // 16, tile, 0)

    low, end = z < Z // 2, jnp.logical_or(z == 0, z == Z - 1)
    inner = jnp.logical_not(end)
    first, last = z == 0, z == Z - 1
    ends = [(rs_way(True, i, first), rs_way(False, i, last)) for i in range(Z - 1)]

    for way in ends[0]:
        way[0]()
    came = [ag_step(1)]
    r1_copy(far(1)).start()
    act(x, z, always)
    for way in ends[0]:
        way[1]()
    act(px, z, always)
    came.append(ag_step(2))
    r1_copy(far(2)).start()
    r1_copy(far(3)).start()
    for way in ends[1]:
        both(way)
    high = jnp.logical_not(low)
    both(rs_way(True, 0, jnp.logical_and(inner, low)))
    both(rs_way(False, 0, jnp.logical_and(inner, high)))
    for s, here in came[0]:
        act(x, s, here)
        act(px, s, here)
    came.append(ag_step(3))
    for way in ends[2]:
        both(way)
    late = (
        rs_way(False, 0, jnp.logical_and(inner, low)),
        rs_way(True, 0, jnp.logical_and(inner, high)),
        rs_way(True, 1, jnp.logical_and(inner, low)),
        rs_way(False, 1, jnp.logical_and(inner, high)),
    )
    for step in (0, 1):
        for way in late:
            way[step]()
    for k in (1, 2):
        for s, here in came[k]:
            act(x, s, here)
            act(px, s, here)

    def out_tile(n, carry):
        xs, r = lax.div(n, tok // rt), lax.rem(n, tok // rt)
        at = pl.ds(pl.multiple_of(r * rt, rt), rt)
        acc = None
        for s in range(Z):
            term = lax.dot_general(
                pre_all[xs, s, at], w[:, s * cols : (s + 1) * cols], (((1,), (1,)), ((), ())),
                preferred_element_type=jnp.float32,
            )
            acc = term if acc is None else acc + term
        for bb in range(nb):
            outp[bb, xs, at] = acc[:, bb * fc : (bb + 1) * fc].astype(jnp.bfloat16)
        return carry

    lax.fori_loop(0, X * (tok // rt), out_tile, 0)

    def op_copy(bb):
        jd = nb * x + bb
        q = lax.rem(j - jd - 1 + J, J)
        return remote(outp.at[bb], outr.at[q], op_s.at[bb], op_r.at[q], {"ja": jd})

    for bb in range(nb):
        pl.when(j != nb * x + bb)(lambda bb=bb: op_copy(bb).start())

    for xs in range(X):
        gt[:, xs * tok : (xs + 1) * tok] = g[xs].T

    n_tiles = Z * (cols // ct)

    def gw_copy(n, slot):
        wide = pl.ds(pl.multiple_of(n * ct, ct), ct)
        return pltpu.make_async_copy(gwt.at[slot], gw.at[:, wide], gws.at[slot])

    def gw_tile(n, carry):
        slot = lax.rem(n, 2)
        s, c = lax.div(n, cols // ct), lax.rem(n, cols // ct)
        at = pl.ds(pl.multiple_of(c * ct, ct), ct)
        pl.when(n >= 2)(lambda: gw_copy(n - 2, slot).wait())
        acc = None
        for xs in range(X):
            term = jnp.dot(
                gt[:, xs * tok : (xs + 1) * tok], pre_all[xs, s, :, at],
                preferred_element_type=jnp.float32,
            )
            acc = term if acc is None else acc + term
        gwt[slot] = acc.astype(jnp.bfloat16)
        gw_copy(n, slot).start()
        return carry

    lax.fori_loop(0, n_tiles, gw_tile, 0)

    def rf_copy():
        return remote(part.at[px, z, rows[1]], rf, rf_s.at[0], rf_r.at[0], to_px)

    for xs in (px, x):
        pl.when(has_left)(lambda xs=xs: take_b(xs, z, z))
        pl.when(has_right)(lambda xs=xs: take_b(xs, z, Z))
        if xs is px:
            rf_copy().start()
    take_1(z)
    pl.when(has_left)(lambda: take_a(z, z))
    pl.when(has_right)(lambda: take_a(z, Z))

    def ox_copy():
        return remote(outp.at[b, px], outx, ox_s.at[0], ox_r.at[0], to_px)

    @pl.when(home)
    def _():
        for q in range(J - 1):
            got(outr.at[q], op_r.at[q])

        def total(xs, r):
            at = pl.ds(pl.multiple_of(r * 16, 16), 16)
            value = outp[b, xs, at].astype(jnp.float32)
            for q in range(J - 1):
                value = value + outr[q, xs, at].astype(jnp.float32)
            return at, value.astype(jnp.bfloat16)

        def far(r, carry):
            at, value = total(px, r)
            outp[b, px, at] = value
            return carry

        def near(r, carry):
            at, value = total(x, r)
            out[at] = value
            return carry

        lax.fori_loop(0, tok // 16, far, 0)
        ox_copy().start()
        lax.fori_loop(0, tok // 16, near, 0)

    pre_in.wait()

    def slope(r, carry):
        at = pl.ds(pl.multiple_of(r * 16, 16), 16)
        value = part[x, z, at].astype(jnp.float32) * gelu_slope(gp[at].astype(jnp.float32))
        gp[at] = value.astype(jnp.bfloat16)
        return carry

    lax.fori_loop(0, ra // 16, slope, 0)
    got(rf, rf_r.at[0])
    add(part.at[x, z, rows[1]], rf, tok - ra)
    lax.fori_loop(ra // 16, tok // 16, slope, 0)

    @pl.when(jnp.logical_not(home))
    def _():
        got(outx, ox_r.at[0])
        out[...] = outx[...]
        go_copy().wait_send()

    @pl.when(home)
    def _():
        ox_copy().wait_send()
        for h in range(X):
            gb_copy(h, 1).wait_send()

    for bb in range(nb):
        pl.when(j != nb * x + bb)(lambda bb=bb: op_copy(bb).wait_send())
    for h in range(X):
        gb_copy(h, 0).wait_send()
    rf_copy().wait_send()
    for d in range(Z):
        r1_copy(d).wait_send()
    for cond, copy in rs_sent + ag_sent[True, id(z)]:
        pl.when(cond)(lambda copy=copy: copy().wait_send())
    for n in range(max(n_tiles - 2, 0), n_tiles):
        gw_copy(n, n % 2).wait()


def stationary(X, J, Z, pre_act, down_weight, grad_out):
    tok, cols = pre_act.shape
    feats, hid = down_weight.shape
    fc = grad_out.shape[1]
    ra = tok * 9 // 16 // 16 * 16
    rb = tok - ra
    ct = 512 if cols % 512 == 0 else 128
    rt = 256 if tok % 256 == 0 else tok
    nb = J // X
    half = jnp.bfloat16
    dma = pltpu.SemaphoreType.DMA
    anywhere = pl.BlockSpec(memory_space=pl.ANY)
    vmem = pl.BlockSpec(memory_space=pltpu.VMEM)
    return pl.pallas_call(
        functools.partial(kernel, X, J, Z, ra, ct, rt),
        out_shape=(
            jax.ShapeDtypeStruct((tok, fc), half),
            jax.ShapeDtypeStruct((tok, cols), half),
            jax.ShapeDtypeStruct((feats, hid), half),
        ),
        in_specs=[anywhere] * 3,
        out_specs=(vmem, vmem, anywhere),
        scratch_shapes=[
            pltpu.VMEM((feats, hid), half),
            pltpu.VMEM((X, Z, tok, cols), half),
            pltpu.VMEM((X, tok, nb * fc), half),
            pltpu.VMEM((nb * fc, X * tok), half),
            pltpu.VMEM((X, Z, tok, cols), half),
            pltpu.VMEM((Z, ra, cols), half),
            pltpu.VMEM((Z + 1, ra, cols), half),
            pltpu.VMEM((X, Z + 1, rb, cols), half),
            pltpu.VMEM((rb, cols), half),
            pltpu.VMEM((nb, X, tok, fc), half),
            pltpu.VMEM((J - 1, X, tok, fc), half),
            pltpu.VMEM((tok, fc), half),
            pltpu.VMEM((2, feats, ct), half),
            dma((4,)), dma((2,)), dma((1,)), dma((1,)), dma((2, X)), dma((2, X)),
            dma((2, X, Z, 3)), dma((2, X, Z)), dma((Z,)), dma((Z,)), dma((Z,)), dma((Z + 1,)),
            dma((X, Z)), dma((X, Z + 1)), dma((1,)), dma((1,)), dma((nb,)), dma((J,)),
            dma((1,)), dma((1,)),
        ],
        compiler_params=pltpu.CompilerParams(
            collective_id=0, has_side_effects=True, vmem_limit_bytes=63 * 2**20
        ),
    )(pre_act, down_weight, grad_out)


def pick(n_ia, n_ja, n_ka):
    def chosen(pre_act, down_weight, grad_out):
        if (n_ia, n_ja, n_ka) == (2, 4, 4) and down_weight.shape[0] > pre_act.shape[0]:
            return stationary(n_ia, n_ja, n_ka, pre_act, down_weight, grad_out)
        return shards(pre_act, down_weight, grad_out)

    return chosen


def solution(mesh):
    placed = (P("ia", ("ja", "ka")), P(("ka", "ia"), "ja"), P("ia", ("ka", "ja")))
    return jax.shard_map(
        pick(mesh.shape["ia"], mesh.shape["ja"], mesh.shape["ka"]),
        mesh=mesh,
        in_specs=placed,
        out_specs=(P("ia", ("ka", "ja")), P("ia", ("ja", "ka")), P(("ka", "ia"), "ja")),
        check_vma=False,
    )
```

```python
import functools

import jax
import jax.numpy as jnp
from jax import lax
from jax.experimental import pallas as pl
from jax.experimental.pallas import tpu as pltpu
from jax.sharding import PartitionSpec as P

MESH = pl.DeviceIdType.MESH
coeff = 0.7978845608028654


def gelu_value(v):
    return 0.5 * v * (1.0 + jnp.tanh(coeff * (v + 0.044715 * v * v * v)))


def gelu_slope(v):
    tval = jnp.tanh(coeff * (v + 0.044715 * v * v * v))
    return 0.5 * (1.0 + tval) + 0.5 * v * (1.0 - tval * tval) * coeff * (
        1.0 + 3.0 * 0.044715 * v * v
    )


def shards(pre_act, down_weight, grad_out):
    pre32 = pre_act.astype(jnp.float32)
    pre_block = lax.all_gather(pre_act, "ka", axis=1, tiled=True)
    hidden = gelu_value(pre_block.astype(jnp.float32)).astype(jnp.bfloat16)
    grad_block = lax.all_gather(grad_out, "ja", axis=1, tiled=True)
    weight_block = lax.all_gather(down_weight, "ia", axis=0, tiled=True)
    out_terms = lax.dot_general(
        hidden, weight_block, (((1,), (1,)), ((), ())), preferred_element_type=jnp.float32
    )
    hidden_terms = jnp.dot(grad_block, weight_block, preferred_element_type=jnp.float32)
    output = lax.psum_scatter(out_terms.astype(jnp.bfloat16), "ja", scatter_dimension=1, tiled=True)
    grad_hidden = lax.psum_scatter(
        hidden_terms.astype(jnp.bfloat16), "ka", scatter_dimension=1, tiled=True
    ).astype(jnp.float32)
    grad_pre = (grad_hidden * gelu_slope(pre32)).astype(jnp.bfloat16)
    weight_terms = lax.dot_general(
        grad_block, hidden, (((0,), (0,)), ((), ())), preferred_element_type=jnp.float32
    )
    grad_weight = lax.psum_scatter(
        weight_terms.astype(jnp.bfloat16), "ia", scatter_dimension=0, tiled=True
    )
    return (output, grad_pre, grad_weight)


def kernel(
    X, J, Z, ra, ct, rt,
    pre, w_hbm, go, out, gp, gw,
    w, pre_all, g, gt, part, r1, rza, rzb, rf, outp, outr, outx, gwt,
    loc, gws, go_s, go_r, gb_s, gb_r, ag_s, ag_r, r1_s, r1_r, ra_s, ra_r, rb_s, rb_r,
    rf_s, rf_r, op_s, op_r, ox_s, ox_r,
):
    x, j, z = lax.axis_index("ia"), lax.axis_index("ja"), lax.axis_index("ka")
    px = 1 - x
    _, _, tok, cols = pre_all.shape
    fc = go.shape[1]
    nb = J // X
    home, b = lax.div(j, nb) == x, lax.rem(j, nb)
    bcols = pl.ds(pl.multiple_of(b * fc, fc), fc)
    to_px, to_right, to_left = {"ia": px}, {"ka": z + 1}, {"ka": z - 1}
    has_left, has_right = z > 0, z < Z - 1
    rows = (pl.ds(0, ra), pl.ds(ra, tok - ra))

    def remote(src, dst, ss, rs, dev):
        return pltpu.make_async_remote_copy(
            src_ref=src, dst_ref=dst, send_sem=ss, recv_sem=rs, device_id=dev, device_id_type=MESH
        )

    def got(dst, rs):
        remote(dst, dst, rs, rs, to_px).wait_recv()

    barrier = pltpu.get_barrier_semaphore()

    def greet(dev):
        pl.semaphore_signal(barrier, inc=1, device_id=dev, device_id_type=MESH)

    greet(to_px)
    for q in range(1, J):
        greet({"ja": lax.rem(j + q, J)})
    pl.when(has_right)(lambda: greet(to_right))
    pl.when(has_left)(lambda: greet(to_left))
    w_in = pltpu.make_async_copy(w_hbm, w, loc.at[0])
    w_in.start()
    own_in = pltpu.make_async_copy(pre, pre_all.at[x, z], loc.at[1])
    own_in.start()
    pre_in = pltpu.make_async_copy(pre, gp, loc.at[2])
    pre_in.start()
    pl.semaphore_wait(barrier, J + has_right.astype(jnp.int32) + has_left.astype(jnp.int32))

    ag_sent = {}
    devs = (to_right, to_left, to_px)

    def ag_send(p, xs, s, t, cond, own=False):
        def copy():
            src = pre.at[rows[p]] if own else pre_all.at[xs, s, rows[p]]
            return remote(
                src, pre_all.at[xs, s, rows[p]], ag_s.at[p, xs, s, t], ag_r.at[p, xs, s], devs[t]
            )

        pl.when(cond)(lambda: copy().start())
        ag_sent.setdefault((xs is x, id(s)), []).append((cond, copy))

    def ag_got(p, xs, s):
        got(pre_all.at[xs, s, rows[p]], ag_r.at[p, xs, s])

    always = z >= 0

    def go_copy():
        return remote(go, g.at[x, :, bcols], go_s.at[0], go_r.at[0], to_px)

    go_in = pltpu.make_async_copy(go, g.at[x, :, bcols], loc.at[3])
    pl.when(jnp.logical_not(home))(lambda: go_copy().start())
    pl.when(home)(lambda: go_in.start())
    ag_send(1, x, z, 2, always, True)
    ag_send(0, x, z, 0, has_right, True)
    ag_send(0, x, z, 1, has_left, True)
    ag_send(0, x, z, 2, always, True)
    ag_send(1, x, z, 0, has_right, True)
    ag_send(1, x, z, 1, has_left, True)

    mate = {"ja": j + 1 - 2 * lax.rem(j, 2)}
    across = {"ja": lax.rem(j + 2, J)}
    ocols = pl.ds(pl.multiple_of((nb - 1 - b) * fc, fc), fc)

    def gb_copy(h, n):
        view = g.at[h, :, bcols]
        return remote(view, view, gb_s.at[n, h], gb_r.at[n, h], (mate, across)[n])

    @pl.when(home)
    def _():
        go_in.wait()
        gb_copy(x, 1).start()
        gb_copy(x, 0).start()
        got(g.at[px, :, bcols], go_r.at[0])
        gb_copy(px, 1).start()
        gb_copy(px, 0).start()

    @pl.when(jnp.logical_not(home))
    def _():
        for h in (x, px):
            got(g.at[h, :, bcols], gb_r.at[1, h])
            gb_copy(h, 0).start()

    ag_got(1, px, z)
    ag_send(1, px, z, 0, has_right)
    ag_send(1, px, z, 1, has_left)

    def ag_step(k):
        sides = ((z - k, z >= k, 0, has_right), (z + k, z + k < Z, 1, has_left))
        for s, came, t, more in sides:
            pl.when(came)(lambda s=s: ag_got(0, x, s))
            ag_send(0, x, s, t, jnp.logical_and(came, more))
            ag_send(0, x, s, 2, came)
            for xs in (x, px):
                pl.when(came)(lambda s=s, xs=xs: ag_got(1, xs, s))
                ag_send(1, xs, s, t, jnp.logical_and(came, more))
        return [(s, came) for s, came, _, _ in sides]

    for h in (x, px):
        got(g.at[h, :, ocols], gb_r.at[0, h])
    w_in.wait()

    def r1_copy(d):
        return remote(part.at[px, d, rows[0]], r1.at[d], r1_s.at[d], r1_r.at[d], to_px)

    def far(i):
        d = 0
        for at in range(Z):
            d = d + jnp.where(z == at, sorted(range(Z), key=lambda o: -abs(o - at))[i], 0)
        return d

    def terms(xs, d):
        def tile(c, carry):
            wide = pl.ds(pl.multiple_of(d * cols + c * ct, ct), ct)
            at = pl.ds(pl.multiple_of(c * ct, ct), ct)
            value = jnp.dot(g[xs], w[:, wide], preferred_element_type=jnp.float32)
            part[xs, d, :, at] = value.astype(jnp.bfloat16)
            return carry

        lax.fori_loop(0, cols // ct, tile, 0)

    terms(px, far(0))
    r1_copy(far(0)).start()
    for i in range(1, Z):
        terms(px, far(i))
    for i in range(Z):
        terms(x, far(i))

    def add(dst, src, count):
        def tile(r, carry):
            at = pl.ds(pl.multiple_of(r * 16, 16), 16)
            value = dst[at].astype(jnp.float32) + src[at].astype(jnp.float32)
            dst[at] = value.astype(jnp.bfloat16)
            return carry

        lax.fori_loop(0, count // 16, tile, 0)

    rs_sent = []

    def take_a(d, slot):
        got(rza.at[slot], ra_r.at[slot])
        add(part.at[x, d, rows[0]], rza.at[slot], ra)

    def take_b(xs, d, slot):
        got(rzb.at[xs, slot], rb_r.at[xs, slot])
        add(part.at[xs, d, rows[1]], rzb.at[xs, slot], tok - ra)

    def take_1(d):
        got(r1.at[d], r1_r.at[d])
        add(part.at[x, d, rows[0]], r1.at[d], ra)

    def rs_way(right, i, cond):
        d = Z - 1 - i if right else i
        cond = jnp.logical_and(cond, d > z if right else d < z)
        more = has_left if right else has_right
        slot = d if right else jnp.where(z == i + 1, Z, i)
        dev = to_right if right else to_left

        def copy_b(xs):
            return remote(
                part.at[xs, d, rows[1]], rzb.at[xs, slot],
                rb_s.at[xs, d], rb_r.at[xs, slot], dev,
            )

        def copy_a():
            return remote(part.at[x, d, rows[0]], rza.at[slot], ra_s.at[d], ra_r.at[slot], dev)

        def part_b():
            for xs in (px, x):

                @pl.when(cond)
                def _():
                    pl.when(more)(lambda: take_b(xs, d, d))
                    copy_b(xs).start()

                rs_sent.append((cond, lambda xs=xs: copy_b(xs)))

        def part_a():
            @pl.when(cond)
            def _():
                take_1(d)
                pl.when(more)(lambda: take_a(d, d))
                copy_a().start()

            rs_sent.append((cond, copy_a))

        return part_b, part_a

    def both(way):
        way[0]()
        way[1]()

    def act(xs, s, cond):
        own = xs is x and s is z

        def tile(r, carry):
            at = pl.ds(pl.multiple_of(r * 16, 16), 16)
            value = gelu_value(pre_all[xs, s, at].astype(jnp.float32))
            pre_all[xs, s, at] = value.astype(jnp.bfloat16)
            return carry

        @pl.when(cond)
        def _():
            for to, copy in () if own else ag_sent[xs is x, id(s)]:
                pl.when(to)(lambda copy=copy: copy().wait_send())
            if xs is px:
                ag_got(0, px, s)
            elif own:
                own_in.wait()
            lax.fori_loop(0, tok // 16, tile, 0)

    n_tiles = cols // ct

    def grad_cols(s, cond):
        def copy(c):
            wide = pl.ds(pl.multiple_of(s * cols + c * ct, ct), ct)
            slot = lax.rem(c, 2)
            return pltpu.make_async_copy(gwt.at[slot], gw.at[:, wide], gws.at[slot])

        def tile(c, carry):
            at = pl.ds(pl.multiple_of(c * ct, ct), ct)
            pl.when(c >= 2)(lambda: copy(c - 2).wait())
            acc = None
            for xs in range(X):
                term = jnp.dot(
                    gt[:, xs * tok : (xs + 1) * tok], pre_all[xs, s, :, at],
                    preferred_element_type=jnp.float32,
                )
                acc = term if acc is None else acc + term
            gwt[lax.rem(c, 2)] = acc.astype(jnp.bfloat16)
            copy(c).start()
            return carry

        @pl.when(cond)
        def _():
            lax.fori_loop(0, n_tiles, tile, 0)
            for c in range(max(n_tiles - 2, 0), n_tiles):
                copy(c).wait()

    low, end = z < Z // 2, jnp.logical_or(z == 0, z == Z - 1)
    inner = jnp.logical_not(end)
    first, last = z == 0, z == Z - 1
    ends = [(rs_way(True, i, first), rs_way(False, i, last)) for i in range(Z - 1)]

    for way in ends[0]:
        way[0]()
    came = [ag_step(1)]
    r1_copy(far(1)).start()
    act(x, z, always)
    for way in ends[0]:
        way[1]()
    act(px, z, always)
    came.append(ag_step(2))
    r1_copy(far(2)).start()
    r1_copy(far(3)).start()
    for way in ends[1]:
        both(way)
    high = jnp.logical_not(low)
    both(rs_way(True, 0, jnp.logical_and(inner, low)))
    both(rs_way(False, 0, jnp.logical_and(inner, high)))
    for s, here in came[0]:
        act(x, s, here)
        act(px, s, here)
    for xs in range(X):
        gt[:, xs * tok : (xs + 1) * tok] = g[xs].T
    grad_cols(z, always)
    for s, here in came[0]:
        grad_cols(s, here)
    for s, here in came[1]:
        act(x, s, jnp.logical_and(here, end))
        act(px, s, jnp.logical_and(here, end))
        grad_cols(s, jnp.logical_and(here, end))
    came.append(ag_step(3))
    for way in ends[2]:
        both(way)
    late = (
        rs_way(False, 0, jnp.logical_and(inner, low)),
        rs_way(True, 0, jnp.logical_and(inner, high)),
        rs_way(True, 1, jnp.logical_and(inner, low)),
        rs_way(False, 1, jnp.logical_and(inner, high)),
    )
    for step in (0, 1):
        for way in late:
            way[step]()
    rest = [(s, jnp.logical_and(here, inner)) for s, here in came[1]] + came[2]
    for s, here in rest:
        act(x, s, here)
        act(px, s, here)

    def out_tile(xs, r):
        at = pl.ds(pl.multiple_of(r * rt, rt), rt)
        acc = None
        for s in range(Z):
            term = lax.dot_general(
                pre_all[xs, s, at], w[:, s * cols : (s + 1) * cols], (((1,), (1,)), ((), ())),
                preferred_element_type=jnp.float32,
            )
            acc = term if acc is None else acc + term
        for bb in range(nb):
            outp[bb, xs, at] = acc[:, bb * fc : (bb + 1) * fc].astype(jnp.bfloat16)

    def op_copy(h, n):
        src = outp.at[(nb - 1 - b, b)[n], h]
        return remote(src, outr.at[n, h], op_s.at[n, h], op_r.at[n, h], (mate, across)[n])

    def both_halves(n, carry):
        h = jnp.where(n == 0, px, x)
        lax.fori_loop(0, tok // rt, lambda r, c: (out_tile(h, r), c)[1], 0)
        op_copy(h, 0).start()
        return carry

    lax.fori_loop(0, X, both_halves, 0)
    for h in (px, x):
        got(outr.at[0, h], op_r.at[0, h])
        add(outp.at[b, h], outr.at[0, h], tok)
        pl.when(jnp.logical_not(home))(lambda h=h: op_copy(h, 1).start())
    for s, here in rest:
        grad_cols(s, here)

    def rf_copy():
        return remote(part.at[px, z, rows[1]], rf, rf_s.at[0], rf_r.at[0], to_px)

    for xs in (px, x):
        pl.when(has_left)(lambda xs=xs: take_b(xs, z, z))
        pl.when(has_right)(lambda xs=xs: take_b(xs, z, Z))
        if xs is px:
            rf_copy().start()
    take_1(z)
    pl.when(has_left)(lambda: take_a(z, z))
    pl.when(has_right)(lambda: take_a(z, Z))

    def ox_copy():
        return remote(outp.at[b, px], outx, ox_s.at[0], ox_r.at[0], to_px)

    @pl.when(home)
    def _():
        got(outr.at[1, px], op_r.at[1, px])
        add(outp.at[b, px], outr.at[1, px], tok)
        ox_copy().start()
        got(outr.at[1, x], op_r.at[1, x])
        add(outp.at[b, x], outr.at[1, x], tok)
        out[...] = outp[b, x]

    pre_in.wait()

    def slope(r, carry):
        at = pl.ds(pl.multiple_of(r * 16, 16), 16)
        value = part[x, z, at].astype(jnp.float32) * gelu_slope(gp[at].astype(jnp.float32))
        gp[at] = value.astype(jnp.bfloat16)
        return carry

    lax.fori_loop(0, ra // 16, slope, 0)
    got(rf, rf_r.at[0])
    add(part.at[x, z, rows[1]], rf, tok - ra)
    lax.fori_loop(ra // 16, tok // 16, slope, 0)

    @pl.when(jnp.logical_not(home))
    def _():
        got(outx, ox_r.at[0])
        out[...] = outx[...]
        go_copy().wait_send()
        for h in range(X):
            op_copy(h, 1).wait_send()

    @pl.when(home)
    def _():
        ox_copy().wait_send()
        for h in range(X):
            gb_copy(h, 1).wait_send()

    for h in range(X):
        op_copy(h, 0).wait_send()
    for h in range(X):
        gb_copy(h, 0).wait_send()
    rf_copy().wait_send()
    for d in range(Z):
        r1_copy(d).wait_send()
    for cond, copy in rs_sent + ag_sent[True, id(z)]:
        pl.when(cond)(lambda copy=copy: copy().wait_send())


def hand_over(pieces, *refs):
    sems = refs[6]
    copies = []
    for n in (2, 1, 0):
        src, dst = refs[n], refs[n + 3]
        step = src.shape[0] // pieces
        for at in range(pieces):
            rows = pl.ds(at * step, step)
            copies.append(pltpu.make_async_copy(src.at[rows], dst.at[rows], sems.at[n, at]))
    for copy in copies:
        copy.start()
    for copy in copies:
        copy.wait()


def stationary(X, J, Z, pre_act, down_weight, grad_out):
    tok, cols = pre_act.shape
    feats, hid = down_weight.shape
    fc = grad_out.shape[1]
    ra = tok * 9 // 16 // 16 * 16
    rb = tok - ra
    ct = 512 if cols % 512 == 0 else 128
    rt = 256 if tok % 256 == 0 else tok
    nb = J // X
    half = jnp.bfloat16
    dma = pltpu.SemaphoreType.DMA
    anywhere = pl.BlockSpec(memory_space=pl.ANY)
    vmem = pl.BlockSpec(memory_space=pltpu.VMEM)
    sums = pl.pallas_call(
        functools.partial(kernel, X, J, Z, ra, ct, rt),
        out_shape=(
            jax.ShapeDtypeStruct((tok, fc), half),
            jax.ShapeDtypeStruct((tok, cols), half),
            jax.ShapeDtypeStruct((feats, hid), half),
        ),
        in_specs=[anywhere] * 3,
        out_specs=(vmem, vmem, anywhere),
        scratch_shapes=[
            pltpu.VMEM((feats, hid), half),
            pltpu.VMEM((X, Z, tok, cols), half),
            pltpu.VMEM((X, tok, nb * fc), half),
            pltpu.VMEM((nb * fc, X * tok), half),
            pltpu.VMEM((X, Z, tok, cols), half),
            pltpu.VMEM((Z, ra, cols), half),
            pltpu.VMEM((Z + 1, ra, cols), half),
            pltpu.VMEM((X, Z + 1, rb, cols), half),
            pltpu.VMEM((rb, cols), half),
            pltpu.VMEM((nb, X, tok, fc), half),
            pltpu.VMEM((2, X, tok, fc), half),
            pltpu.VMEM((tok, fc), half),
            pltpu.VMEM((2, feats, ct), half),
            dma((4,)), dma((2,)), dma((1,)), dma((1,)), dma((2, X)), dma((2, X)),
            dma((2, X, Z, 3)), dma((2, X, Z)), dma((Z,)), dma((Z,)), dma((Z,)), dma((Z + 1,)),
            dma((X, Z)), dma((X, Z + 1)), dma((1,)), dma((1,)), dma((2, X)), dma((2, X)),
            dma((1,)), dma((1,)),
        ],
        compiler_params=pltpu.CompilerParams(
            collective_id=0, has_side_effects=True, vmem_limit_bytes=63 * 2**20
        ),
    )(pre_act, down_weight, grad_out)
    pieces = 8
    return pl.pallas_call(
        functools.partial(hand_over, pieces),
        out_shape=tuple(jax.ShapeDtypeStruct(a.shape, a.dtype) for a in sums),
        in_specs=[anywhere] * 3,
        out_specs=(anywhere,) * 3,
        scratch_shapes=[dma((3, pieces))],
        compiler_params=pltpu.CompilerParams(vmem_limit_bytes=63 * 2**20),
    )(*sums)


def pick(n_ia, n_ja, n_ka):
    def chosen(pre_act, down_weight, grad_out):
        if (n_ia, n_ja, n_ka) == (2, 4, 4) and down_weight.shape[0] > pre_act.shape[0]:
            return stationary(n_ia, n_ja, n_ka, pre_act, down_weight, grad_out)
        return shards(pre_act, down_weight, grad_out)

    return chosen


def solution(mesh):
    placed = (P("ia", ("ja", "ka")), P(("ka", "ia"), "ja"), P("ia", ("ka", "ja")))
    return jax.shard_map(
        pick(mesh.shape["ia"], mesh.shape["ja"], mesh.shape["ka"]),
        mesh=mesh,
        in_specs=placed,
        out_specs=(P("ia", ("ka", "ja")), P("ia", ("ja", "ka")), P(("ka", "ia"), "ja")),
        check_vma=False,
    )
```

```python
import functools

import jax
import jax.numpy as jnp
from jax import lax
from jax.experimental import pallas as pl
from jax.experimental.pallas import tpu as pltpu
from jax.sharding import PartitionSpec as P

MESH = pl.DeviceIdType.MESH
coeff = 0.7978845608028654


def gelu_value(v):
    return 0.5 * v * (1.0 + jnp.tanh(coeff * (v + 0.044715 * v * v * v)))


def gelu_slope(v):
    tval = jnp.tanh(coeff * (v + 0.044715 * v * v * v))
    return 0.5 * (1.0 + tval) + 0.5 * v * (1.0 - tval * tval) * coeff * (
        1.0 + 3.0 * 0.044715 * v * v
    )


def shards(pre_act, down_weight, grad_out):
    pre32 = pre_act.astype(jnp.float32)
    pre_block = lax.all_gather(pre_act, "ka", axis=1, tiled=True)
    hidden = gelu_value(pre_block.astype(jnp.float32)).astype(jnp.bfloat16)
    grad_block = lax.all_gather(grad_out, "ja", axis=1, tiled=True)
    weight_block = lax.all_gather(down_weight, "ia", axis=0, tiled=True)
    out_terms = lax.dot_general(
        hidden, weight_block, (((1,), (1,)), ((), ())), preferred_element_type=jnp.float32
    )
    hidden_terms = jnp.dot(grad_block, weight_block, preferred_element_type=jnp.float32)
    output = lax.psum_scatter(out_terms.astype(jnp.bfloat16), "ja", scatter_dimension=1, tiled=True)
    grad_hidden = lax.psum_scatter(
        hidden_terms.astype(jnp.bfloat16), "ka", scatter_dimension=1, tiled=True
    ).astype(jnp.float32)
    grad_pre = (grad_hidden * gelu_slope(pre32)).astype(jnp.bfloat16)
    weight_terms = lax.dot_general(
        grad_block, hidden, (((0,), (0,)), ((), ())), preferred_element_type=jnp.float32
    )
    grad_weight = lax.psum_scatter(
        weight_terms.astype(jnp.bfloat16), "ia", scatter_dimension=0, tiled=True
    )
    return (output, grad_pre, grad_weight)


def kernel(
    X, J, Z, ra, ct, rt,
    pre, w_hbm, go, out, gp, gw,
    w, pre_all, g, gt, part, r1, rza, rzb, rf, outa, outp, outr, outx, gwt,
    loc, gws, go_s, go_r, gb_s, gb_r, ag_s, ag_r, r1_s, r1_r, ra_s, ra_r, rb_s, rb_r,
    rf_s, rf_r, op_s, op_r, ox_s, ox_r,
):
    x, j, z = lax.axis_index("ia"), lax.axis_index("ja"), lax.axis_index("ka")
    px = 1 - x
    _, _, tok, cols = pre_all.shape
    fc = go.shape[1]
    nb = J // X
    home, b = lax.div(j, nb) == x, lax.rem(j, nb)
    bcols = pl.ds(pl.multiple_of(b * fc, fc), fc)
    to_px, to_right, to_left = {"ia": px}, {"ka": z + 1}, {"ka": z - 1}
    has_left, has_right = z > 0, z < Z - 1
    rows = (pl.ds(0, ra), pl.ds(ra, tok - ra))

    def remote(src, dst, ss, rs, dev):
        return pltpu.make_async_remote_copy(
            src_ref=src, dst_ref=dst, send_sem=ss, recv_sem=rs, device_id=dev, device_id_type=MESH
        )

    def got(dst, rs):
        remote(dst, dst, rs, rs, to_px).wait_recv()

    barrier = pltpu.get_barrier_semaphore()

    def greet(dev):
        pl.semaphore_signal(barrier, inc=1, device_id=dev, device_id_type=MESH)

    greet(to_px)
    for q in range(1, J):
        greet({"ja": lax.rem(j + q, J)})
    pl.when(has_right)(lambda: greet(to_right))
    pl.when(has_left)(lambda: greet(to_left))
    w_in = pltpu.make_async_copy(w_hbm, w, loc.at[0])
    w_in.start()
    own_in = pltpu.make_async_copy(pre, pre_all.at[x, z], loc.at[1])
    own_in.start()
    pre_in = pltpu.make_async_copy(pre, gp, loc.at[2])
    pre_in.start()
    pl.semaphore_wait(barrier, J + has_right.astype(jnp.int32) + has_left.astype(jnp.int32))

    ag_sent = {}
    devs = (to_right, to_left, to_px)

    def ag_send(p, xs, s, t, cond, own=False):
        def copy():
            src = pre.at[rows[p]] if own else pre_all.at[xs, s, rows[p]]
            return remote(
                src, pre_all.at[xs, s, rows[p]], ag_s.at[p, xs, s, t], ag_r.at[p, xs, s], devs[t]
            )

        pl.when(cond)(lambda: copy().start())
        ag_sent.setdefault((xs is x, id(s)), []).append((cond, copy))

    def ag_got(p, xs, s):
        got(pre_all.at[xs, s, rows[p]], ag_r.at[p, xs, s])

    always = z >= 0

    def go_copy():
        return remote(go, g.at[x, :, bcols], go_s.at[0], go_r.at[0], to_px)

    go_in = pltpu.make_async_copy(go, g.at[x, :, bcols], loc.at[3])
    pl.when(jnp.logical_not(home))(lambda: go_copy().start())
    pl.when(home)(lambda: go_in.start())
    ag_send(1, x, z, 2, always, True)
    ag_send(0, x, z, 0, has_right, True)
    ag_send(0, x, z, 1, has_left, True)
    ag_send(0, x, z, 2, always, True)
    ag_send(1, x, z, 0, has_right, True)
    ag_send(1, x, z, 1, has_left, True)

    mate = {"ja": j + 1 - 2 * lax.rem(j, 2)}
    across = {"ja": lax.rem(j + 2, J)}
    ocols = pl.ds(pl.multiple_of((nb - 1 - b) * fc, fc), fc)

    def gb_copy(h, n):
        view = g.at[h, :, bcols]
        return remote(view, view, gb_s.at[n, h], gb_r.at[n, h], (mate, across)[n])

    @pl.when(home)
    def _():
        go_in.wait()
        gb_copy(x, 1).start()
        gb_copy(x, 0).start()
        got(g.at[px, :, bcols], go_r.at[0])
        gb_copy(px, 1).start()
        gb_copy(px, 0).start()

    @pl.when(jnp.logical_not(home))
    def _():
        for h in (x, px):
            got(g.at[h, :, bcols], gb_r.at[1, h])
            gb_copy(h, 0).start()

    ag_got(1, px, z)
    ag_send(1, px, z, 0, has_right)
    ag_send(1, px, z, 1, has_left)

    def ag_step(k):
        sides = ((z - k, z >= k, 0, has_right), (z + k, z + k < Z, 1, has_left))
        for s, came, t, more in sides:
            pl.when(came)(lambda s=s: ag_got(0, x, s))
            ag_send(0, x, s, t, jnp.logical_and(came, more))
            ag_send(0, x, s, 2, came)
            for xs in (x, px):
                pl.when(came)(lambda s=s, xs=xs: ag_got(1, xs, s))
                ag_send(1, xs, s, t, jnp.logical_and(came, more))
        return [(s, came) for s, came, _, _ in sides]

    for h in (x, px):
        got(g.at[h, :, ocols], gb_r.at[0, h])
    w_in.wait()

    def r1_copy(d):
        return remote(part.at[px, d, rows[0]], r1.at[d], r1_s.at[d], r1_r.at[d], to_px)

    def far(i):
        d = 0
        for at in range(Z):
            d = d + jnp.where(z == at, sorted(range(Z), key=lambda o: -abs(o - at))[i], 0)
        return d

    def terms(xs, d):
        def tile(c, carry):
            wide = pl.ds(pl.multiple_of(d * cols + c * ct, ct), ct)
            at = pl.ds(pl.multiple_of(c * ct, ct), ct)
            value = jnp.dot(g[xs], w[:, wide], preferred_element_type=jnp.float32)
            part[xs, d, :, at] = value.astype(jnp.bfloat16)
            return carry

        lax.fori_loop(0, cols // ct, tile, 0)

    terms(px, far(0))
    r1_copy(far(0)).start()
    for i in range(1, Z):
        terms(px, far(i))
    for i in range(Z):
        terms(x, far(i))

    def add(dst, src, count):
        def tile(r, carry):
            at = pl.ds(pl.multiple_of(r * 16, 16), 16)
            value = dst[at].astype(jnp.float32) + src[at].astype(jnp.float32)
            dst[at] = value.astype(jnp.bfloat16)
            return carry

        lax.fori_loop(0, count // 16, tile, 0)

    rs_sent = []

    def take_a(d, slot):
        got(rza.at[slot], ra_r.at[slot])
        add(part.at[x, d, rows[0]], rza.at[slot], ra)

    def take_b(xs, d, slot):
        got(rzb.at[xs, slot], rb_r.at[xs, slot])
        add(part.at[xs, d, rows[1]], rzb.at[xs, slot], tok - ra)

    def take_1(d):
        got(r1.at[d], r1_r.at[d])
        add(part.at[x, d, rows[0]], r1.at[d], ra)

    def rs_way(right, i, cond):
        d = Z - 1 - i if right else i
        cond = jnp.logical_and(cond, d > z if right else d < z)
        more = has_left if right else has_right
        slot = d if right else jnp.where(z == i + 1, Z, i)
        dev = to_right if right else to_left

        def copy_b(xs):
            return remote(
                part.at[xs, d, rows[1]], rzb.at[xs, slot],
                rb_s.at[xs, d], rb_r.at[xs, slot], dev,
            )

        def copy_a():
            return remote(part.at[x, d, rows[0]], rza.at[slot], ra_s.at[d], ra_r.at[slot], dev)

        def part_b():
            for xs in (px, x):

                @pl.when(cond)
                def _():
                    pl.when(more)(lambda: take_b(xs, d, d))
                    copy_b(xs).start()

                rs_sent.append((cond, lambda xs=xs: copy_b(xs)))

        def part_a():
            @pl.when(cond)
            def _():
                take_1(d)
                pl.when(more)(lambda: take_a(d, d))
                copy_a().start()

            rs_sent.append((cond, copy_a))

        return part_b, part_a

    def both(way):
        way[0]()
        way[1]()

    def act(xs, s, cond):
        own = xs is x and s is z

        def tile(r, carry):
            at = pl.ds(pl.multiple_of(r * 16, 16), 16)
            value = gelu_value(pre_all[xs, s, at].astype(jnp.float32))
            pre_all[xs, s, at] = value.astype(jnp.bfloat16)
            return carry

        @pl.when(cond)
        def _():
            for to, copy in () if own else ag_sent[xs is x, id(s)]:
                pl.when(to)(lambda copy=copy: copy().wait_send())
            if xs is px:
                ag_got(0, px, s)
            elif own:
                own_in.wait()
            lax.fori_loop(0, tok // 16, tile, 0)

    n_tiles = cols // ct

    def grad_cols(s, cond):
        def copy(c):
            wide = pl.ds(pl.multiple_of(s * cols + c * ct, ct), ct)
            slot = lax.rem(c, 2)
            return pltpu.make_async_copy(gwt.at[slot], gw.at[:, wide], gws.at[slot])

        def tile(c, carry):
            at = pl.ds(pl.multiple_of(c * ct, ct), ct)
            pl.when(c >= 2)(lambda: copy(c - 2).wait())
            acc = None
            for xs in range(X):
                term = jnp.dot(
                    gt[:, xs * tok : (xs + 1) * tok], pre_all[xs, s, :, at],
                    preferred_element_type=jnp.float32,
                )
                acc = term if acc is None else acc + term
            gwt[lax.rem(c, 2)] = acc.astype(jnp.bfloat16)
            copy(c).start()
            return carry

        @pl.when(cond)
        def _():
            lax.fori_loop(0, n_tiles, tile, 0)
            for c in range(max(n_tiles - 2, 0), n_tiles):
                copy(c).wait()

    low, end = z < Z // 2, jnp.logical_or(z == 0, z == Z - 1)
    inner = jnp.logical_not(end)
    early, last_s = jnp.where(low, 0, Z - 1), jnp.where(low, Z - 1, 0)

    def out_term(xs, at, s):
        wide = pl.ds(pl.multiple_of(s * cols, cols), cols)
        return lax.dot_general(
            pre_all[xs, s, at], w[:, wide], (((1,), (1,)), ((), ())),
            preferred_element_type=jnp.float32,
        )

    def out_early(cond):
        def tile(n, carry):
            xs, r = lax.div(n, tok // rt), lax.rem(n, tok // rt)
            at = pl.ds(pl.multiple_of(r * rt, rt), rt)
            acc = out_term(xs, at, early)
            for s in range(1, Z - 1):
                acc = acc + out_term(xs, at, s)
            outa[xs, at] = acc
            return carry

        @pl.when(cond)
        def _():
            lax.fori_loop(0, X * (tok // rt), tile, 0)

    first, last = z == 0, z == Z - 1
    ends = [(rs_way(True, i, first), rs_way(False, i, last)) for i in range(Z - 1)]

    for way in ends[0]:
        way[0]()
    came = [ag_step(1)]
    r1_copy(far(1)).start()
    act(x, z, always)
    for way in ends[0]:
        way[1]()
    act(px, z, always)
    came.append(ag_step(2))
    r1_copy(far(2)).start()
    r1_copy(far(3)).start()
    for way in ends[1]:
        both(way)
    high = jnp.logical_not(low)
    both(rs_way(True, 0, jnp.logical_and(inner, low)))
    both(rs_way(False, 0, jnp.logical_and(inner, high)))
    for s, here in came[0]:
        act(x, s, here)
        act(px, s, here)
    for xs in range(X):
        gt[:, xs * tok : (xs + 1) * tok] = g[xs].T
    grad_cols(z, always)
    for s, here in came[0]:
        grad_cols(s, here)
    for s, here in came[1]:
        act(x, s, jnp.logical_and(here, end))
        act(px, s, jnp.logical_and(here, end))
        grad_cols(s, jnp.logical_and(here, end))
    out_early(end)
    came.append(ag_step(3))
    for way in ends[2]:
        both(way)
    late = (
        rs_way(False, 0, jnp.logical_and(inner, low)),
        rs_way(True, 0, jnp.logical_and(inner, high)),
        rs_way(True, 1, jnp.logical_and(inner, low)),
        rs_way(False, 1, jnp.logical_and(inner, high)),
    )
    for step in (0, 1):
        for way in late:
            way[step]()
    out_early(inner)
    rest = [(s, jnp.logical_and(here, inner)) for s, here in came[1]] + came[2]
    for s, here in rest:
        act(x, s, here)
        act(px, s, here)

    def out_tile(xs, r):
        at = pl.ds(pl.multiple_of(r * rt, rt), rt)
        acc = outa[xs, at] + out_term(xs, at, last_s)
        for bb in range(nb):
            outp[bb, xs, at] = acc[:, bb * fc : (bb + 1) * fc].astype(jnp.bfloat16)

    def op_copy(h, n):
        src = outp.at[(nb - 1 - b, b)[n], h]
        return remote(src, outr.at[n, h], op_s.at[n, h], op_r.at[n, h], (mate, across)[n])

    def both_halves(n, carry):
        h = jnp.where(n == 0, px, x)
        lax.fori_loop(0, tok // rt, lambda r, c: (out_tile(h, r), c)[1], 0)
        op_copy(h, 0).start()
        return carry

    lax.fori_loop(0, X, both_halves, 0)
    for h in (px, x):
        got(outr.at[0, h], op_r.at[0, h])
        add(outp.at[b, h], outr.at[0, h], tok)
        pl.when(jnp.logical_not(home))(lambda h=h: op_copy(h, 1).start())
    for s, here in rest:
        grad_cols(s, here)

    def rf_copy():
        return remote(part.at[px, z, rows[1]], rf, rf_s.at[0], rf_r.at[0], to_px)

    for xs in (px, x):
        pl.when(has_left)(lambda xs=xs: take_b(xs, z, z))
        pl.when(has_right)(lambda xs=xs: take_b(xs, z, Z))
        if xs is px:
            rf_copy().start()
    take_1(z)
    pl.when(has_left)(lambda: take_a(z, z))
    pl.when(has_right)(lambda: take_a(z, Z))

    pre_in.wait()

    def slope(r, carry):
        at = pl.ds(pl.multiple_of(r * 16, 16), 16)
        value = part[x, z, at].astype(jnp.float32) * gelu_slope(gp[at].astype(jnp.float32))
        gp[at] = value.astype(jnp.bfloat16)
        return carry

    lax.fori_loop(0, ra // 16, slope, 0)
    def ox_copy():
        return remote(outp.at[b, px], outx, ox_s.at[0], ox_r.at[0], to_px)

    @pl.when(home)
    def _():
        got(outr.at[1, px], op_r.at[1, px])
        add(outp.at[b, px], outr.at[1, px], tok)
        ox_copy().start()
        got(outr.at[1, x], op_r.at[1, x])
        add(outp.at[b, x], outr.at[1, x], tok)
        out[...] = outp[b, x]

    got(rf, rf_r.at[0])
    add(part.at[x, z, rows[1]], rf, tok - ra)
    lax.fori_loop(ra // 16, tok // 16, slope, 0)

    @pl.when(jnp.logical_not(home))
    def _():
        got(outx, ox_r.at[0])
        out[...] = outx[...]
        go_copy().wait_send()
        for h in range(X):
            op_copy(h, 1).wait_send()

    @pl.when(home)
    def _():
        ox_copy().wait_send()
        for h in range(X):
            gb_copy(h, 1).wait_send()

    for h in range(X):
        op_copy(h, 0).wait_send()
    for h in range(X):
        gb_copy(h, 0).wait_send()
    rf_copy().wait_send()
    for d in range(Z):
        r1_copy(d).wait_send()
    for cond, copy in rs_sent + ag_sent[True, id(z)]:
        pl.when(cond)(lambda copy=copy: copy().wait_send())


def hand_over(pieces, *refs):
    held, sems = refs[6:9], refs[9]
    copies = []
    for n in (2, 1, 0):
        src, dst, mid = refs[n], refs[n + 3], held[n]
        step = src.shape[0] // pieces
        for at in range(pieces):
            rows = pl.ds(at * step, step)
            come = pltpu.make_async_copy(src.at[rows], mid.at[rows], sems.at[0, n, at])
            leave = pltpu.make_async_copy(mid.at[rows], dst.at[rows], sems.at[1, n, at])
            copies.append((come, leave))
    for come, _ in copies:
        come.start()
    for come, leave in copies:
        come.wait()
        leave.start()
    for _, leave in copies:
        leave.wait()


def stationary(X, J, Z, pre_act, down_weight, grad_out):
    tok, cols = pre_act.shape
    feats, hid = down_weight.shape
    fc = grad_out.shape[1]
    ra = tok * 9 // 16 // 16 * 16
    rb = tok - ra
    ct = 512 if cols % 512 == 0 else 128
    rt = 256 if tok % 256 == 0 else tok
    nb = J // X
    half = jnp.bfloat16
    dma = pltpu.SemaphoreType.DMA
    anywhere = pl.BlockSpec(memory_space=pl.ANY)
    vmem = pl.BlockSpec(memory_space=pltpu.VMEM)
    sums = pl.pallas_call(
        functools.partial(kernel, X, J, Z, ra, ct, rt),
        out_shape=(
            jax.ShapeDtypeStruct((tok, fc), half),
            jax.ShapeDtypeStruct((tok, cols), half),
            jax.ShapeDtypeStruct((feats, hid), half),
        ),
        in_specs=[anywhere] * 3,
        out_specs=(vmem, vmem, anywhere),
        scratch_shapes=[
            pltpu.VMEM((feats, hid), half),
            pltpu.VMEM((X, Z, tok, cols), half),
            pltpu.VMEM((X, tok, nb * fc), half),
            pltpu.VMEM((nb * fc, X * tok), half),
            pltpu.VMEM((X, Z, tok, cols), half),
            pltpu.VMEM((Z, ra, cols), half),
            pltpu.VMEM((Z + 1, ra, cols), half),
            pltpu.VMEM((X, Z + 1, rb, cols), half),
            pltpu.VMEM((rb, cols), half),
            pltpu.VMEM((X, tok, nb * fc), jnp.float32),
            pltpu.VMEM((nb, X, tok, fc), half),
            pltpu.VMEM((2, X, tok, fc), half),
            pltpu.VMEM((tok, fc), half),
            pltpu.VMEM((2, feats, ct), half),
            dma((4,)), dma((2,)), dma((1,)), dma((1,)), dma((2, X)), dma((2, X)),
            dma((2, X, Z, 3)), dma((2, X, Z)), dma((Z,)), dma((Z,)), dma((Z,)), dma((Z + 1,)),
            dma((X, Z)), dma((X, Z + 1)), dma((1,)), dma((1,)), dma((2, X)), dma((2, X)),
            dma((1,)), dma((1,)),
        ],
        compiler_params=pltpu.CompilerParams(
            collective_id=0, has_side_effects=True, vmem_limit_bytes=63 * 2**20
        ),
    )(pre_act, down_weight, grad_out)
    pieces = 8
    return pl.pallas_call(
        functools.partial(hand_over, pieces),
        out_shape=tuple(jax.ShapeDtypeStruct(a.shape, a.dtype) for a in sums),
        in_specs=[anywhere] * 3,
        out_specs=(anywhere,) * 3,
        scratch_shapes=[pltpu.VMEM(a.shape, a.dtype) for a in sums] + [dma((2, 3, pieces))],
        compiler_params=pltpu.CompilerParams(vmem_limit_bytes=63 * 2**20),
    )(*sums)


def pick(n_ia, n_ja, n_ka):
    def chosen(pre_act, down_weight, grad_out):
        if (n_ia, n_ja, n_ka) == (2, 4, 4) and down_weight.shape[0] > pre_act.shape[0]:
            return stationary(n_ia, n_ja, n_ka, pre_act, down_weight, grad_out)
        return shards(pre_act, down_weight, grad_out)

    return chosen


def solution(mesh):
    placed = (P("ia", ("ja", "ka")), P(("ka", "ia"), "ja"), P("ia", ("ka", "ja")))
    return jax.shard_map(
        pick(mesh.shape["ia"], mesh.shape["ja"], mesh.shape["ka"]),
        mesh=mesh,
        in_specs=placed,
        out_specs=(P("ia", ("ka", "ja")), P("ia", ("ja", "ka")), P(("ka", "ia"), "ja")),
        check_vma=False,
    )
```
